256 devices in a mesh: src: 16 (over z, y_hi), space: 16 (over y_lo, x, core).
Axes of the slice: x: 4, y: 4 (y_hi: 2, y_lo: 2; y = y_hi * 2 + y_lo), z: 8, core: 2. Of those that a mesh axis runs over, the one named last changes fastest.
Arguments:
- wavefield: float32 [16, 9, 128, 64, 128], P('src', None, 'space'), may hold values from -6 to 6
- strain_bank: bfloat16 [16, 6, 128, 64, 128], P('src', None, 'space'), may hold values from -6 to 6
- owners: int32 [4], replicated, may hold values from 0 to 15, as said below
- region: int32 [128, 64, 128], P('space'), may hold values from 0 to 7
- region_lambda: float32 [8], replicated, may hold values from 1 to 2
- region_mu: float32 [8], replicated, may hold values from 0.5 to 1
- region_buoyancy: float32 [8], replicated, may hold values from 0.5 to 1
Outputs:
- new_wavefield: float32 [16, 9, 128, 64, 128], P('src', None, 'space')
- lambda_kernel: float32 [128, 64, 128], P('space', 'src')
- mu_kernel: float32 [128, 64, 128], P('space', 'src')
The draws below stay inside these ranges and needn't reach their ends.
Inputs may be any that keep to these rules, and one draw needn't show every extreme that they name: `owners`: 4 distinct owner indices in an order drawn per run; 0 and 15 are always among them.
All inputs are finite; a program needn't handle non-finite values.
Results may differ from the reference program's by a relative error of at most 0.0003.
Values may be sent and summed in bfloat16 or wider, within the bound.
No kernel may reach another device: no remote copies, remote signals or barrier semaphores. Data moves between devices by JAX's collectives and lax.ppermute only.
A program may use at most 128 MiB of HBM per device.

```python
import jax
import jax.numpy as jnp
from jax import lax

NY = 64
NZ = 128
STEPS = 4
REGIONS = 8
SOURCES = 16
OWNERS = 16
NX = 128


def draw_owners(key, part):
    first_key, second_key = jax.random.split(jax.random.fold_in(key, 17))
    middle = jax.random.permutation(first_key, OWNERS - 2) + 1
    chosen = jnp.concatenate([jnp.array([0, OWNERS - 1], dtype=jnp.int32), middle[:STEPS - 2].astype(jnp.int32)])
    return jax.random.permutation(second_key, chosen).astype(jnp.int32)


def place_ends(entries, stream_key, smallest, largest):
    shape = entries.shape
    place = [jax.random.randint(jax.random.fold_in(stream_key, axis), (), 0, shape[axis]) for axis in range(len(shape))]
    entries = entries.at[tuple(place)].set(smallest)
    longest = shape.index(max(shape))
    place[longest] = (place[longest] + 1) % shape[longest]
    return entries.at[tuple(place)].set(largest)


def block_levels(own_key, shape, shards, smallest, top_value):
    def one(position, shards_of):
        steps = jax.random.uniform(jax.random.fold_in(jax.random.fold_in(own_key, 6), position), (shards_of,), jnp.float32, smallest / len(shards), top_value / len(shards))
        return jnp.repeat(jnp.exp(steps), shape[position] // shards_of).reshape((-1,) + (1,) * (len(shape) - position - 1))

    gain = one(*shards[0])
    for cut in shards[1:]:
        gain = gain * one(*cut)
    return gain


def scatter_about(own_key, shape, deviation, bound, cuts=(), held_as=jnp.bfloat16):
    level = block_levels(own_key, shape, cuts, -0.22, 0.18) if cuts else 1.0
    drawn = jax.random.normal(own_key, shape, jnp.float32) * deviation * level
    return jnp.minimum(jnp.maximum(drawn, -bound), bound).astype(held_as)


def setup_inputs(seed: int = 0) -> dict:
    streams_of = jax.random.split(jax.random.key(seed), 8)
    return {
        "wavefield": scatter_about(streams_of[0], (SOURCES, 9, NX, NY, NZ), 1.0, 6.0, ((0, 16), (2, 16)), jnp.float32),
        "strain_bank": scatter_about(streams_of[1], (OWNERS, 6, NX, NY, NZ), 1.0, 6.0, ((0, 16), (2, 16))),
        "owners": draw_owners(jax.random.fold_in(streams_of[7], 71), 0),
        "region": place_ends(jax.random.randint(streams_of[3], (NX, NY, NZ), 0, REGIONS), jax.random.fold_in(streams_of[3], 1), 0, REGIONS - 1).astype(jnp.int32),
        "region_lambda": jnp.clip(jax.random.uniform(streams_of[4], (REGIONS,), jnp.float32, 1.0, 2.0), 1.0, 2.0),
        "region_mu": jnp.clip(jax.random.uniform(streams_of[5], (REGIONS,), jnp.float32, 0.5, 1.0), 0.5, 1.0),
        "region_buoyancy": jnp.clip(jax.random.uniform(streams_of[6], (REGIONS,), jnp.float32, 0.5, 1.0), 0.5, 1.0),
    }


step_size = 0.3
x_force_terms = (0, 5, 4)
y_force_terms = (5, 1, 3)
z_force_terms = (4, 3, 2)


def slab_of(values, along, start, length):
    slicer = [slice(None)] * values.ndim
    slicer[values.ndim + along] = slice(start, start + length)
    return values[tuple(slicer)]


def diff_valid(padded, along):
    length = padded.shape[along] - 4
    near = slab_of(padded, along, 3, length) - slab_of(padded, along, 1, length)
    far = slab_of(padded, along, 4, length) - slab_of(padded, along, 0, length)
    return (8.0 * near - far) / 12.0


def diff_zero(values, along):
    widths = [(0, 0)] * values.ndim
    widths[values.ndim + along] = (2, 2)
    return diff_valid(jnp.pad(values, widths), along)


def component(values, which):
    return values[..., which, :, :, :]


def pick_terms(values, order):
    return jnp.stack([component(values, which) for which in order], -4)


def stress_update(stress, grad_x, grad_y, grad_z, lame_first, shear):
    diagonal = [component(grad_x, 0), component(grad_y, 1), component(grad_z, 2)]
    divergence = diagonal[0] + diagonal[1] + diagonal[2]
    parts = [component(stress, which) + step_size * (lame_first * divergence + 2.0 * shear * diagonal[which]) for which in range(3)]
    parts.append(component(stress, 3) + step_size * shear * (component(grad_z, 1) + component(grad_y, 2)))
    parts.append(component(stress, 4) + step_size * shear * (component(grad_z, 0) + component(grad_x, 2)))
    parts.append(component(stress, 5) + step_size * shear * (component(grad_y, 0) + component(grad_x, 1)))
    return jnp.stack(parts, -4)


def correlate(stress, receiver, lame_first, shear):
    trace = component(stress, 0) + component(stress, 1) + component(stress, 2)
    theta = trace / (3.0 * lame_first + 2.0 * shear)
    recv_trace = receiver[0] + receiver[1] + receiver[2]
    term_lambda = step_size * theta * recv_trace
    inner = jnp.zeros_like(theta)
    for which in range(3):
        inner = inner + (component(stress, which) - lame_first * theta) / (2.0 * shear) * receiver[which]
    for which in range(3, 6):
        inner = inner + component(stress, which) / shear * receiver[which]
    term_mu = step_size * 2.0 * inner
    return term_lambda, term_mu


def reference(wavefield, strain_bank, owners, region, region_lambda, region_mu, region_buoyancy):
    lame_first = region_lambda[region]
    shear = region_mu[region]
    buoyancy = region_buoyancy[region]

    def one_source(carry, state):
        kernel_lambda, kernel_mu = carry
        for time_step in range(STEPS):
            velocity = state[0:3]
            stress = state[3:9]
            force = diff_zero(pick_terms(stress, x_force_terms), -3) + diff_zero(pick_terms(stress, y_force_terms), -2) + diff_zero(pick_terms(stress, z_force_terms), -1)
            velocity = velocity + step_size * buoyancy * force
            stress = stress_update(stress, diff_zero(velocity, -3), diff_zero(velocity, -2), diff_zero(velocity, -1), lame_first, shear)
            state = jnp.concatenate([velocity, stress], -4)
            receiver = lax.dynamic_index_in_dim(strain_bank, owners[time_step], 0, keepdims=False).astype(jnp.float32)
            term_lambda, term_mu = correlate(stress, receiver, lame_first, shear)
            kernel_lambda = kernel_lambda + term_lambda
            kernel_mu = kernel_mu + term_mu
        return (kernel_lambda, kernel_mu), state

    zeros = jnp.zeros(region.shape, jnp.float32)
    (kernel_lambda, kernel_mu), new_wavefield = lax.scan(one_source, (zeros, zeros), wavefield)
    return new_wavefield, kernel_lambda, kernel_mu
```

```python
import functools

import jax
import jax.numpy as jnp
from jax import lax
from jax.experimental import pallas as pl
from jax.experimental.pallas import tpu as pltpu
from jax.sharding import PartitionSpec as P

STEPS = 4
DT = 0.3
SRC = 16
ZS = 8
NX, NY, NZ = 8, 64, 128
REGIONS = 8
F32 = jnp.float32
BF16 = jnp.bfloat16

WIDE = (0, 4, 5)
FORCE = ((0, 5, 4), (5, 1, 3), (4, 3, 2))

DEPTH = [6, 6, 6] + [8 if comp in WIDE else 6 for comp in range(6)]
EXACT = 2
TOP = {}
for _field in range(9):
    for _d in range(1, DEPTH[_field] + 1):
        TOP[_field, _d] = len(TOP)
REST = {}
for _field in range(9):
    for _d in range(1, EXACT + 1):
        REST[_field, _d] = len(TOP) + len(REST)
MESSAGE = len(TOP) + len(REST)
LABELS = 6

VMEM = pl.BlockSpec(memory_space=pltpu.VMEM)
SMEM = pl.BlockSpec(memory_space=pltpu.SMEM)


def params(mib):
    return pltpu.CompilerParams(vmem_limit_bytes=mib * 2**20)


def shape(*dims, dtype=F32):
    return jax.ShapeDtypeStruct(dims, dtype)


def lookup(region, table):
    value = jnp.full(region.shape, table[0], F32)
    for label in range(1, REGIONS):
        value = jnp.where(region == label, table[label], value)
    return value


def put_row(message, field, d, value):
    top = value.astype(BF16)
    message[TOP[field, d]] = top
    if d <= EXACT:
        message[REST[field, d]] = (value - top.astype(F32)).astype(BF16)


def get_row(message, field, d):
    value = message[TOP[field, d]].astype(F32)
    if d <= EXACT:
        value = value + message[REST[field, d]].astype(F32)
    return value


def put_edges(to_low, to_high, field, x, value, low, high):
    if x < DEPTH[field]:
        put_row(to_low, field, x + 1, value * low)
    if NX - x <= DEPTH[field]:
        put_row(to_high, field, NX - x, value * high)


def pack_kernel(flags, region, state, to_low, to_high):
    low, high = flags[0], flags[1]
    for field in range(9):
        for x in range(NX):
            put_edges(to_low, to_high, field, x, state[field, x], low, high)
    for d in range(1, LABELS + 1):
        to_low[MESSAGE + d - 1] = ((region[d - 1] + 1).astype(F32) * low).astype(BF16)
        to_high[MESSAGE + d - 1] = ((region[NX - d] + 1).astype(F32) * high).astype(BF16)


def bank_kernel(bank, slabs):
    for x in range(NX):
        for comp in range(6):
            for half in range(2):
                slabs[x * 2 + half, comp] = bank[comp, x, half * 32 : half * 32 + 32]


def material_kernel(tables, region, below, above, bu, lam_step, mu_step):
    tab = [[tables[k, i] * (DT / 12.0) for i in range(REGIONS)] for k in range(3)]
    for x in range(-6, NX + 6):
        if 0 <= x < NX:
            label = (region[x] + 1).astype(F32)
        elif x < 0:
            label = below[MESSAGE - x - 1].astype(F32)
        else:
            label = above[MESSAGE + x - NX].astype(F32)
        zero = jnp.zeros((NY, NZ), F32)
        values = [zero, zero, zero]
        for i in range(REGIONS):
            here = label == float(i + 1)
            values = [jnp.where(here, tab[k][i], values[k]) for k in range(3)]
        lam_step[x + 6] = values[0]
        mu_step[x + 6] = values[1]
        bu[x + 6] = values[2]


def shift_y(f, k):
    zero = jnp.zeros((abs(k), f.shape[1]), f.dtype)
    if k > 0:
        return jnp.concatenate([f[k:], zero], 0)
    return jnp.concatenate([zero, f[: f.shape[0] + k]], 0)


def diff_y(f):
    return 8.0 * (shift_y(f, 1) - shift_y(f, -1)) - (shift_y(f, 2) - shift_y(f, -2))


def diff_z(f, band):
    top = f.astype(BF16)
    rest = (f - top.astype(F32)).astype(BF16)
    return jnp.dot(jnp.concatenate([top, rest], 1), band, preferred_element_type=F32)


def double_kernel(last, flags, state, below, above, bu, lam_step, mu_step, band_ref, mid, out, *rest):
    if last:
        v1, s1, v2 = rest
    else:
        to_low, to_high, v1, s1, v2 = rest
        low, high = flags[0], flags[1]
    band = band_ref[...]

    def start(field, x):
        if 0 <= x < NX:
            return state[field, x]
        return get_row(below, field, -x) if x < 0 else get_row(above, field, x - NX + 1)

    def stress0(comp, x):
        return start(3 + comp, x)

    def velocity0(comp, x):
        return start(comp, x)

    def velocity1(comp, x):
        return v1[comp, x + 6]

    def stress1(comp, x):
        if 0 <= x < NX:
            return mid[comp, x]
        return s1[comp, x + 4] if x < 0 else s1[comp, x - NX + 4]

    def velocity2(comp, x):
        if 0 <= x < NX:
            return out[comp, x]
        return v2[comp, x + 2] if x < 0 else v2[comp, 2 + x - NX]

    def diff_x(field, comp, x):
        return 8.0 * (field(comp, x + 1) - field(comp, x - 1)) - (field(comp, x + 2) - field(comp, x - 2))

    def new_velocity(velocity, stress, x):
        b = bu[x + 6]
        for comp, (cx, cy, cz) in enumerate(FORCE):
            force = diff_x(stress, cx, x) + diff_y(stress(cy, x)) + diff_z(stress(cz, x), band)
            yield comp, velocity(comp, x) + b * force

    def new_stress(stress, velocity, x):
        lam, mu = lam_step[x + 6], mu_step[x + 6]
        v = [velocity(comp, x) for comp in range(3)]
        dx = [diff_x(velocity, comp, x) for comp in range(3)]
        dy = [diff_y(v[comp]) for comp in range(3)]
        dz = [diff_z(v[comp], band) for comp in range(3)]
        common = lam * (dx[0] + dy[1] + dz[2])
        twice = mu + mu
        return [
            stress(0, x) + (common + twice * dx[0]),
            stress(1, x) + (common + twice * dy[1]),
            stress(2, x) + (common + twice * dz[2]),
            stress(3, x) + mu * (dz[1] + dy[2]),
            stress(4, x) + mu * (dz[0] + dx[2]),
            stress(5, x) + mu * (dy[0] + dx[1]),
        ]

    for x in range(-6, NX + 6):
        for comp, new in new_velocity(velocity0, stress0, x):
            v1[comp, x + 6] = new
    for x in range(-4, NX + 4):
        for comp, new in enumerate(new_stress(stress0, velocity1, x)):
            if 0 <= x < NX:
                mid[comp, x] = new
            elif x < 0:
                s1[comp, x + 4] = new
            else:
                s1[comp, x - NX + 4] = new
    for x in range(-2, NX + 2):
        for comp, new in new_velocity(velocity1, stress1, x):
            if 0 <= x < NX:
                out[comp, x] = new
                if not last:
                    put_edges(to_low, to_high, comp, x, new, low, high)
            elif x < 0:
                v2[comp, x + 2] = new
            else:
                v2[comp, 2 + x - NX] = new
    for x in range(NX):
        for comp, new in enumerate(new_stress(stress1, velocity2, x)):
            out[3 + comp, x] = new
            if not last:
                put_edges(to_low, to_high, 3 + comp, x, new, low, high)


def correlate_kernel(place, *refs):
    states = refs[:STEPS]
    parts = refs[STEPS : STEPS + ZS]
    out = refs[-1]
    z, half = place[0], place[1]
    lower = lax.broadcasted_iota(jnp.int32, (8, NZ), 0) < 4
    for k in range(ZS):
        x = lax.rem(z + ZS - k, ZS)
        for e in range(2):
            which = half if e == 0 else 1 - half
            y0 = pl.multiple_of(which * 32, 32)
            p = jnp.zeros((32, NZ), F32)
            q = jnp.zeros((32, NZ), F32)
            for t in range(STEPS):
                skip = 3 * (t % 2)
                s = [states[t][skip + comp, x, pl.ds(y0, 32), :] for comp in range(6)]
                r = [parts[k][e, t, comp].astype(F32) for comp in range(6)]
                p = p + (s[0] + s[1] + s[2]) * (r[0] + r[1] + r[2])
                diag = s[0] * r[0] + s[1] * r[1] + s[2] * r[2]
                off = s[3] * r[3] + s[4] * r[4] + s[5] * r[5]
                q = q + diag + (off + off)
            for g in range(4):
                pv, qv = p[g * 8 : g * 8 + 8], q[g * 8 : g * 8 + 8]
                d = which * 8 + g * 2
                out[d, x] = jnp.where(lower, pv, pltpu.roll(qv, 4, 0))
                out[d + 1, x] = jnp.where(lower, pltpu.roll(pv, 4, 0), qv)


def finish_kernel(tables, place, region, terms, k_lambda, k_mu):
    src = place[2]
    tab = [[tables[k, i] for i in range(REGIONS)] for k in range(2)]
    group = pl.multiple_of((src // 2) * 8, 8)
    upper = lax.broadcasted_iota(jnp.int32, (8, NZ), 0) >= 4
    flip = jnp.where(upper, 1, 0) != src % 2
    for x in range(NX):
        total = terms[0, x]
        for s in range(1, SRC):
            total = total + terms[s, x]
        reg = region[x, pl.ds(group, 8), :]
        reg = jnp.where(flip, pltpu.roll(reg, 4, 0), reg)
        lame, shear = lookup(reg, tab[0]), lookup(reg, tab[1])
        theta = total / (3.0 * lame + 2.0 * shear)
        k_lambda[x] = (DT * theta)[:4]
        mu_term = (pltpu.roll(total, 4, 0) - lame * theta) * (DT / shear)
        k_mu[x] = mu_term[:4]


def src_moves(dz, dy):
    moves = []
    for z in range(ZS):
        for y in range(2):
            moves.append((z * 2 + y, ((z + dz) % ZS) * 2 + (y ^ dy)))
    return moves


def gather_receivers(slabs, owners):
    slabs = lax.all_to_all(slabs, "src", 0, 0, tiled=True)
    mine = jnp.stack([lax.dynamic_index_in_dim(slabs, owners[t], 0, keepdims=False) for t in range(STEPS)])
    other = lax.ppermute(mine, "src", src_moves(0, 1))
    pair = jnp.stack([mine, other])
    parts = [pair] + [None] * (ZS - 1)
    up = down = pair
    for k in range(1, 5):
        up = lax.ppermute(up, "src", src_moves(1, 0))
        parts[k] = up
        if k < 4:
            down = lax.ppermute(down, "src", src_moves(-1, 0))
            parts[ZS - k] = down
    return parts


def exchange(to_low, to_high):
    n = lax.axis_size("space")
    below = lax.ppermute(to_high, "space", [(i, (i + 1) % n) for i in range(n)])
    above = lax.ppermute(to_low, "space", [((i + 1) % n, i) for i in range(n)])
    return below, above


def local(wavefield, strain_bank, owners, region, region_lambda, region_mu, region_buoyancy):
    n = lax.axis_size("space")
    pos = lax.axis_index("space")
    src = lax.axis_index("src")
    flags = jnp.stack([(pos > 0).astype(F32), (pos < n - 1).astype(F32)])
    place = jnp.stack([src // 2, src % 2, src]).astype(jnp.int32)
    tables = jnp.stack([region_lambda, region_mu, region_buoyancy])
    eye = functools.partial(jnp.eye, NZ, dtype=F32)
    band = 8.0 * (eye(k=-1) - eye(k=1)) - (eye(k=-2) - eye(k=2))
    band = jnp.concatenate([band, band], 0).astype(BF16)
    state = wavefield[0]

    to_low, to_high = pl.pallas_call(
        pack_kernel,
        out_shape=[shape(MESSAGE + LABELS, NY, NZ, dtype=BF16)] * 2,
        in_specs=[SMEM, VMEM, VMEM],
        out_specs=[VMEM] * 2,
        compiler_params=params(12),
        name="pack",
    )(flags, region, state)
    slabs = pl.pallas_call(
        bank_kernel,
        out_shape=shape(SRC, 6, 32, NZ, dtype=BF16),
        in_specs=[VMEM],
        out_specs=VMEM,
        compiler_params=params(8),
        cost_estimate=pl.CostEstimate(flops=1_000_000, bytes_accessed=40_000_000, transcendentals=0),
        name="bank",
    )(strain_bank[0])
    parts = gather_receivers(slabs, owners)

    states = []
    for pair in range(STEPS // 2):
        below, above = exchange(to_low, to_high)
        if pair == 0:
            bu, lam_step, mu_step = pl.pallas_call(
                material_kernel,
                out_shape=[shape(NX + 12, NY, NZ)] * 3,
                in_specs=[SMEM, VMEM, VMEM, VMEM],
                out_specs=[VMEM] * 3,
                compiler_params=params(12),
                name="material",
            )(tables, region, below, above)
        last = pair == STEPS // 2 - 1
        outs = [shape(6, NX, NY, NZ), shape(9, NX, NY, NZ)]
        outs += [] if last else [shape(MESSAGE, NY, NZ, dtype=BF16)] * 2
        mid, state, *messages = pl.pallas_call(
            functools.partial(double_kernel, last),
            out_shape=outs,
            in_specs=[SMEM] + [VMEM] * 7,
            out_specs=[VMEM] * len(outs),
            scratch_shapes=[
                pltpu.VMEM((3, NX + 12, NY, NZ), F32),
                pltpu.VMEM((6, 8, NY, NZ), F32),
                pltpu.VMEM((3, 4, NY, NZ), F32),
            ],
            compiler_params=params(20),
            cost_estimate=pl.CostEstimate(flops=40_000_000, bytes_accessed=20_000_000, transcendentals=0),
            name="double",
        )(flags, state, below, above, bu, lam_step, mu_step, band)
        if not last:
            to_low, to_high = messages
        states += [mid, state]

    terms = pl.pallas_call(
        correlate_kernel,
        out_shape=shape(SRC, NX, 8, NZ),
        in_specs=[SMEM] + [VMEM] * (STEPS + ZS),
        out_specs=VMEM,
        compiler_params=params(18),
        name="correlate",
    )(place, *states, *parts)

    total = lax.all_to_all(terms, "src", 0, 0, tiled=True)
    kernel_lambda, kernel_mu = pl.pallas_call(
        finish_kernel,
        out_shape=[shape(NX, NY // SRC, NZ)] * 2,
        in_specs=[SMEM, SMEM, VMEM, VMEM],
        out_specs=[VMEM] * 2,
        compiler_params=params(12),
        name="finish",
    )(tables, place, region, total)
    return state[None], kernel_lambda, kernel_mu


def solution(mesh):
    in_specs = (
        P("src", None, "space", None, None),
        P("src", None, "space", None, None),
        P(),
        P("space", None, None),
        P(),
        P(),
        P(),
    )
    out_specs = (
        P("src", None, "space", None, None),
        P("space", "src", None),
        P("space", "src", None),
    )
    return jax.shard_map(local, mesh=mesh, in_specs=in_specs, out_specs=out_specs, check_vma=False)
```

```python
import functools

import jax
import jax.numpy as jnp
from jax import lax
from jax.experimental import pallas as pl
from jax.experimental.pallas import tpu as pltpu
from jax.sharding import PartitionSpec as P

STEPS = 4
DT = 0.3
SRC = 16
ZS = 8
NX, NY, NZ = 8, 64, 128
REGIONS = 8
F32 = jnp.float32
BF16 = jnp.bfloat16

WIDE = (0, 4, 5)
FORCE = ((0, 5, 4), (5, 1, 3), (4, 3, 2))

DEPTH = [6, 6, 6] + [8 if comp in WIDE else 6 for comp in range(6)]
EXACT = 2
TOP = {}
for _field in range(9):
    for _d in range(1, DEPTH[_field] + 1):
        TOP[_field, _d] = len(TOP)
REST = {}
for _field in range(9):
    for _d in range(1, EXACT + 1):
        REST[_field, _d] = len(TOP) + len(REST)
MESSAGE = len(TOP) + len(REST)
LABELS = 6

VMEM = pl.BlockSpec(memory_space=pltpu.VMEM)
SMEM = pl.BlockSpec(memory_space=pltpu.SMEM)
ANY = pl.BlockSpec(memory_space=pl.ANY)
DMA = pltpu.SemaphoreType.DMA


def params(mib):
    return pltpu.CompilerParams(vmem_limit_bytes=mib * 2**20)


def shape(*dims, dtype=F32):
    return jax.ShapeDtypeStruct(dims, dtype)


def lookup(region, table):
    value = jnp.full(region.shape, table[0], F32)
    for label in range(1, REGIONS):
        value = jnp.where(region == label, table[label], value)
    return value


def put_row(message, field, d, value):
    top = value.astype(BF16)
    message[TOP[field, d]] = top
    if d <= EXACT:
        message[REST[field, d]] = (value - top.astype(F32)).astype(BF16)


def get_row(message, field, d):
    value = message[TOP[field, d]].astype(F32)
    if d <= EXACT:
        value = value + message[REST[field, d]].astype(F32)
    return value


def put_edges(to_low, to_high, field, x, value, low, high):
    if x < DEPTH[field]:
        put_row(to_low, field, x + 1, value * low)
    if NX - x <= DEPTH[field]:
        put_row(to_high, field, NX - x, value * high)


def pack_kernel(flags, region, state, to_low, to_high):
    low, high = flags[0], flags[1]
    for field in range(9):
        for x in range(NX):
            put_edges(to_low, to_high, field, x, state[field, x], low, high)
    for d in range(1, LABELS + 1):
        to_low[MESSAGE + d - 1] = ((region[d - 1] + 1).astype(F32) * low).astype(BF16)
        to_high[MESSAGE + d - 1] = ((region[NX - d] + 1).astype(F32) * high).astype(BF16)


def bank_kernel(bank, slabs):
    for x in range(NX):
        for comp in range(6):
            for half in range(2):
                slabs[x * 2 + half, comp] = bank[comp, x, half * 32 : half * 32 + 32]


def material_kernel(tables, region, below, above, bu, lam_step, mu_step):
    tab = [[tables[k, i] * (DT / 12.0) for i in range(REGIONS)] for k in range(3)]
    for x in range(-6, NX + 6):
        if 0 <= x < NX:
            label = (region[x] + 1).astype(F32)
        elif x < 0:
            label = below[MESSAGE - x - 1].astype(F32)
        else:
            label = above[MESSAGE + x - NX].astype(F32)
        zero = jnp.zeros((NY, NZ), F32)
        values = [zero, zero, zero]
        for i in range(REGIONS):
            here = label == float(i + 1)
            values = [jnp.where(here, tab[k][i], values[k]) for k in range(3)]
        lam_step[x + 6] = values[0]
        mu_step[x + 6] = values[1]
        bu[x + 6] = values[2]


def shift_y(f, k):
    zero = jnp.zeros((abs(k), f.shape[1]), f.dtype)
    if k > 0:
        return jnp.concatenate([f[k:], zero], 0)
    return jnp.concatenate([zero, f[: f.shape[0] + k]], 0)


def diff_y(f):
    return 8.0 * (shift_y(f, 1) - shift_y(f, -1)) - (shift_y(f, 2) - shift_y(f, -2))


def diff_z(f, band):
    top = f.astype(BF16)
    rest = (f - top.astype(F32)).astype(BF16)
    return jnp.dot(jnp.concatenate([top, rest], 1), band, preferred_element_type=F32)


def double_kernel(last, flags, state, below, above, bu, lam_step, mu_step, band_ref, mid, out, *rest):
    if last:
        v1, s1, v2 = rest
    else:
        to_low, to_high, v1, s1, v2 = rest
        low, high = flags[0], flags[1]
    band = band_ref[...]

    def start(field, x):
        if 0 <= x < NX:
            return state[field, x]
        return get_row(below, field, -x) if x < 0 else get_row(above, field, x - NX + 1)

    def stress0(comp, x):
        return start(3 + comp, x)

    def velocity0(comp, x):
        return start(comp, x)

    def velocity1(comp, x):
        return v1[comp, x + 6]

    def stress1(comp, x):
        if 0 <= x < NX:
            return mid[comp, x]
        return s1[comp, x + 4] if x < 0 else s1[comp, x - NX + 4]

    def velocity2(comp, x):
        if 0 <= x < NX:
            return out[comp, x]
        return v2[comp, x + 2] if x < 0 else v2[comp, 2 + x - NX]

    def diff_x(field, comp, x):
        return 8.0 * (field(comp, x + 1) - field(comp, x - 1)) - (field(comp, x + 2) - field(comp, x - 2))

    def new_velocity(velocity, stress, x):
        b = bu[x + 6]
        for comp, (cx, cy, cz) in enumerate(FORCE):
            force = diff_x(stress, cx, x) + diff_y(stress(cy, x)) + diff_z(stress(cz, x), band)
            yield comp, velocity(comp, x) + b * force

    def new_stress(stress, velocity, x):
        lam, mu = lam_step[x + 6], mu_step[x + 6]
        v = [velocity(comp, x) for comp in range(3)]
        dx = [diff_x(velocity, comp, x) for comp in range(3)]
        dy = [diff_y(v[comp]) for comp in range(3)]
        dz = [diff_z(v[comp], band) for comp in range(3)]
        common = lam * (dx[0] + dy[1] + dz[2])
        twice = mu + mu
        return [
            stress(0, x) + (common + twice * dx[0]),
            stress(1, x) + (common + twice * dy[1]),
            stress(2, x) + (common + twice * dz[2]),
            stress(3, x) + mu * (dz[1] + dy[2]),
            stress(4, x) + mu * (dz[0] + dx[2]),
            stress(5, x) + mu * (dy[0] + dx[1]),
        ]

    for x in range(-6, NX + 6):
        for comp, new in new_velocity(velocity0, stress0, x):
            v1[comp, x + 6] = new
    for x in range(-4, NX + 4):
        for comp, new in enumerate(new_stress(stress0, velocity1, x)):
            if 0 <= x < NX:
                mid[comp, x] = new
            elif x < 0:
                s1[comp, x + 4] = new
            else:
                s1[comp, x - NX + 4] = new
    for x in range(-2, NX + 2):
        for comp, new in new_velocity(velocity1, stress1, x):
            if 0 <= x < NX:
                out[comp, x] = new
                if not last:
                    put_edges(to_low, to_high, comp, x, new, low, high)
            elif x < 0:
                v2[comp, x + 2] = new
            else:
                v2[comp, 2 + x - NX] = new
    for x in range(NX):
        for comp, new in enumerate(new_stress(stress1, velocity2, x)):
            out[3 + comp, x] = new
            if not last:
                put_edges(to_low, to_high, 3 + comp, x, new, low, high)


def correlate(z, half, turns, states, parts, stress, strain, sems, emit):
    lower = lax.broadcasted_iota(jnp.int32, (8, NZ), 0) < 4
    rows = [lax.rem(z + ZS - k, ZS) for k in turns]
    copies = []
    for n, x in enumerate(rows):
        group = [
            pltpu.make_async_copy(states[t].at[pl.ds(3 * (t % 2), 6), x], stress.at[n, t], sems.at[n, t])
            for t in range(STEPS)
        ]
        for e in range(len(parts[n])):
            target = strain.at[n, e] if len(parts[n]) == 2 else strain.at[n]
            group.append(pltpu.make_async_copy(parts[n][e], target, sems.at[n, STEPS + e]))
        copies.append(group)
        for copy in group:
            copy.start()
    for n, x in enumerate(rows):
        for copy in copies[n]:
            copy.wait()
        for e in range(2):
            which = half if e == 0 else 1 - half
            y0 = pl.multiple_of(which * 32, 32)
            p = jnp.zeros((32, NZ), F32)
            q = jnp.zeros((32, NZ), F32)
            for t in range(STEPS):
                s = [stress[n, t, comp, pl.ds(y0, 32), :] for comp in range(6)]
                r = [strain[n, e, t, comp].astype(F32) for comp in range(6)]
                p = p + (s[0] + s[1] + s[2]) * (r[0] + r[1] + r[2])
                diag = s[0] * r[0] + s[1] * r[1] + s[2] * r[2]
                off = s[3] * r[3] + s[4] * r[4] + s[5] * r[5]
                q = q + diag + (off + off)
            for g in range(4):
                pv, qv = p[g * 8 : g * 8 + 8], q[g * 8 : g * 8 + 8]
                d = which * 8 + g * 2
                emit(d, x, jnp.where(lower, pv, pltpu.roll(qv, 4, 0)))
                emit(d + 1, x, jnp.where(lower, pltpu.roll(pv, 4, 0), qv))


LAST_TURN = 4
TURNS = tuple(k for k in range(ZS) if k != LAST_TURN)


def correlate_kernel(place, *refs):
    states, parts = refs[:STEPS], refs[STEPS : STEPS + len(TURNS)]
    terms, stress, strain, sems = refs[STEPS + len(TURNS) :]

    def emit(d, x, value):
        terms[d, x] = value

    for d in range(SRC):
        terms[d, lax.rem(place[0] + ZS - LAST_TURN, ZS)] = jnp.zeros((8, NZ), F32)
    correlate(place[0], place[1], TURNS, states, [(part,) for part in parts], stress, strain, sems, emit)


def last_correlate_kernel(place, *refs):
    states, part = refs[:STEPS], refs[STEPS : STEPS + 2]
    terms, stress, strain, mine, sems, sem = refs[STEPS + 3 :]

    def emit(d, x, value):
        mine[d] = value

    correlate(place[0], place[1], (LAST_TURN,), states, [part], stress, strain, sems, emit)
    row = lax.rem(place[0] + ZS - LAST_TURN, ZS)
    copy = pltpu.make_async_copy(mine, terms.at[:, row], sem)
    copy.start()
    copy.wait()


def correlate_scratch(turns):
    return [
        pltpu.VMEM((turns, STEPS, 6, NY, NZ), F32),
        pltpu.VMEM((turns, 2, STEPS, 6, 32, NZ), BF16),
    ]


def finish_kernel(tables, place, region, terms, k_lambda, k_mu):
    src = place[2]
    tab = [[tables[k, i] for i in range(REGIONS)] for k in range(2)]
    group = pl.multiple_of((src // 2) * 8, 8)
    upper = lax.broadcasted_iota(jnp.int32, (8, NZ), 0) >= 4
    flip = jnp.where(upper, 1, 0) != src % 2
    for x in range(NX):
        total = terms[0, x]
        for s in range(1, SRC):
            total = total + terms[s, x]
        reg = region[x, pl.ds(group, 8), :]
        reg = jnp.where(flip, pltpu.roll(reg, 4, 0), reg)
        lame, shear = lookup(reg, tab[0]), lookup(reg, tab[1])
        theta = total / (3.0 * lame + 2.0 * shear)
        k_lambda[x] = (DT * theta)[:4]
        mu_term = (pltpu.roll(total, 4, 0) - lame * theta) * (DT / shear)
        k_mu[x] = mu_term[:4]


def src_moves(dz, dy):
    moves = []
    for z in range(ZS):
        for y in range(2):
            moves.append((z * 2 + y, ((z + dz) % ZS) * 2 + (y ^ dy)))
    return moves


def hold_kernel(value, after, same):
    pass


def hold(value, after):
    return pl.pallas_call(
        hold_kernel,
        out_shape=shape(*value.shape, dtype=value.dtype),
        in_specs=[ANY, ANY],
        out_specs=ANY,
        input_output_aliases={0: 0},
        name="hold",
    )(value, after)


def start_gather(slabs, owners):
    slabs = lax.all_to_all(slabs, "src", 0, 0, tiled=True)
    mine = jnp.stack([lax.dynamic_index_in_dim(slabs, owners[t], 0, keepdims=False) for t in range(STEPS)])
    other = lax.ppermute(mine, "src", src_moves(0, 1))
    pair = jnp.stack([mine, other])
    parts = [pair] + [None] * (ZS - 1)
    up = down = pair
    for k in range(1, 4):
        parts[k] = up = lax.ppermute(up, "src", src_moves(1, 0))
        parts[ZS - k] = down = lax.ppermute(down, "src", src_moves(-1, 0))
    return parts


def end_gather(parts, after):
    first = lax.ppermute(hold(parts[3][0], after), "src", src_moves(1, 0))
    second = lax.ppermute(hold(parts[5][1], after), "src", src_moves(-1, 0))
    return first, second


def exchange(to_low, to_high):
    n = lax.axis_size("space")
    below = lax.ppermute(to_high, "space", [(i, (i + 1) % n) for i in range(n)])
    above = lax.ppermute(to_low, "space", [((i + 1) % n, i) for i in range(n)])
    return below, above


def local(wavefield, strain_bank, owners, region, region_lambda, region_mu, region_buoyancy):
    n = lax.axis_size("space")
    pos = lax.axis_index("space")
    src = lax.axis_index("src")
    flags = jnp.stack([(pos > 0).astype(F32), (pos < n - 1).astype(F32)])
    place = jnp.stack([src // 2, src % 2, src]).astype(jnp.int32)
    tables = jnp.stack([region_lambda, region_mu, region_buoyancy])
    eye = functools.partial(jnp.eye, NZ, dtype=F32)
    band = 8.0 * (eye(k=-1) - eye(k=1)) - (eye(k=-2) - eye(k=2))
    band = jnp.concatenate([band, band], 0).astype(BF16)
    state = wavefield[0]

    to_low, to_high = pl.pallas_call(
        pack_kernel,
        out_shape=[shape(MESSAGE + LABELS, NY, NZ, dtype=BF16)] * 2,
        in_specs=[SMEM, VMEM, VMEM],
        out_specs=[VMEM] * 2,
        compiler_params=params(12),
        name="pack",
    )(flags, region, state)
    slabs = pl.pallas_call(
        bank_kernel,
        out_shape=shape(SRC, 6, 32, NZ, dtype=BF16),
        in_specs=[VMEM],
        out_specs=VMEM,
        compiler_params=params(8),
        cost_estimate=pl.CostEstimate(flops=1_000_000, bytes_accessed=40_000_000, transcendentals=0),
        name="bank",
    )(strain_bank[0])
    parts = start_gather(slabs, owners)

    states = []
    for pair in range(STEPS // 2):
        below, above = exchange(to_low, to_high)
        if pair == 0:
            bu, lam_step, mu_step = pl.pallas_call(
                material_kernel,
                out_shape=[shape(NX + 12, NY, NZ)] * 3,
                in_specs=[SMEM, VMEM, VMEM, VMEM],
                out_specs=[VMEM] * 3,
                compiler_params=params(12),
                name="material",
            )(tables, region, below, above)
        last = pair == STEPS // 2 - 1
        outs = [shape(6, NX, NY, NZ), shape(9, NX, NY, NZ)]
        outs += [] if last else [shape(MESSAGE, NY, NZ, dtype=BF16)] * 2
        mid, state, *messages = pl.pallas_call(
            functools.partial(double_kernel, last),
            out_shape=outs,
            in_specs=[SMEM] + [VMEM] * 7,
            out_specs=[VMEM] * len(outs),
            scratch_shapes=[
                pltpu.VMEM((3, NX + 12, NY, NZ), F32),
                pltpu.VMEM((6, 8, NY, NZ), F32),
                pltpu.VMEM((3, 4, NY, NZ), F32),
            ],
            compiler_params=params(20),
            cost_estimate=pl.CostEstimate(flops=40_000_000, bytes_accessed=20_000_000, transcendentals=0),
            name="double",
        )(flags, state, below, above, bu, lam_step, mu_step, band)
        if not last:
            to_low, to_high = messages
        states += [mid, state]

    halves = end_gather(parts, state)
    terms = pl.pallas_call(
        correlate_kernel,
        out_shape=shape(SRC, NX, 8, NZ),
        in_specs=[SMEM] + [ANY] * (STEPS + len(TURNS)),
        out_specs=VMEM,
        scratch_shapes=correlate_scratch(len(TURNS)) + [DMA((len(TURNS), STEPS + 2))],
        compiler_params=params(58),
        cost_estimate=pl.CostEstimate(flops=8_000_000, bytes_accessed=12_000_000, transcendentals=0),
        name="correlate",
    )(place, *states, *[parts[k] for k in TURNS])
    terms = pl.pallas_call(
        last_correlate_kernel,
        out_shape=shape(SRC, NX, 8, NZ),
        in_specs=[SMEM] + [ANY] * (STEPS + 3),
        out_specs=ANY,
        scratch_shapes=correlate_scratch(1) + [pltpu.VMEM((SRC, 8, NZ), F32), DMA((1, STEPS + 2)), DMA],
        input_output_aliases={STEPS + 3: 0},
        compiler_params=params(58),
        name="last_correlate",
    )(place, *states, *halves, terms)

    total = lax.all_to_all(terms, "src", 0, 0, tiled=True)
    kernel_lambda, kernel_mu = pl.pallas_call(
        finish_kernel,
        out_shape=[shape(NX, NY // SRC, NZ)] * 2,
        in_specs=[SMEM, SMEM, VMEM, VMEM],
        out_specs=[VMEM] * 2,
        compiler_params=params(12),
        name="finish",
    )(tables, place, region, total)
    return state[None], kernel_lambda, kernel_mu


def solution(mesh):
    in_specs = (
        P("src", None, "space", None, None),
        P("src", None, "space", None, None),
        P(),
        P("space", None, None),
        P(),
        P(),
        P(),
    )
    out_specs = (
        P("src", None, "space", None, None),
        P("space", "src", None),
        P("space", "src", None),
    )
    return jax.shard_map(local, mesh=mesh, in_specs=in_specs, out_specs=out_specs, check_vma=False)
```
